128 devices in a mesh: ctx: 2 (over core), expert: 64 (over z, x, y).
Axes of the slice: x: 4, y: 4, z: 4, core: 2. Of those that a mesh axis runs over, the one named last changes fastest.
Arguments:
- tokens: bfloat16 [64, 256, 2048], P('expert', 'ctx'), may hold values from -6 to 6
- positions: int32 [64, 256], P('expert'), may hold values from 0 to 191, as said below
- routes: int32 [64, 256, 8], P('expert', 'ctx'), may hold values from 0 to 127, all different within a row; in each aligned block of 128 rows (0 to 127, 128 to 255, ..., all dimensions but the last counted through in order) at most 8 rows name the same one
- attn_gain: bfloat16 [2048], P(('ctx', 'expert')), may hold values from 0.5 to 1.5
- w_query: bfloat16 [2048, 4096], P(('ctx', 'expert')), may hold values from -0.125 to 0.125
- w_key: bfloat16 [2048, 512], P(('ctx', 'expert')), may hold values from -0.125 to 0.125
- w_value: bfloat16 [2048, 512], P(('ctx', 'expert')), may hold values from -0.125 to 0.125
- query_gain: bfloat16 [128], P(('ctx', 'expert')), may hold values from 0.099609375 to 1.8984375
- key_gain: bfloat16 [128], P(('ctx', 'expert')), may hold values from 0.099609375 to 1.8984375
- w_out: bfloat16 [4096, 2048], P(('ctx', 'expert')), may hold values from -0.375 to 0.375
- ffn_gain: bfloat16 [2048], P(('ctx', 'expert')), may hold values from 0.5 to 1.5
- w_router: bfloat16 [2048, 128], P(('ctx', 'expert')), may hold values from -0.0625 to 0.0625
- w_gate: bfloat16 [128, 2048, 768], P(('ctx', 'expert')), may hold values from -0.125 to 0.125
- w_up: bfloat16 [128, 2048, 768], P(('ctx', 'expert')), may hold values from -0.125 to 0.125
- w_down: bfloat16 [128, 768, 2048], P(('ctx', 'expert')), may hold values from -0.875 to 0.875
- cotangent: bfloat16 [64, 256, 2048], P('expert', 'ctx'), may hold values from -6 to 6
Outputs:
- block_out: float32 [64, 256, 2048], P('expert', 'ctx')
- d_tokens: float32 [64, 256, 2048], P('expert', 'ctx')
- d_attn_gain: float32 [2048], P(('ctx', 'expert'))
- d_w_query: float32 [2048, 4096], P(('ctx', 'expert'))
- d_w_key: float32 [2048, 512], P(('ctx', 'expert'))
- d_w_value: float32 [2048, 512], P(('ctx', 'expert'))
- d_query_gain: float32 [128], P(('ctx', 'expert'))
- d_key_gain: float32 [128], P(('ctx', 'expert'))
- d_w_out: float32 [4096, 2048], P(('ctx', 'expert'))
- d_ffn_gain: float32 [2048], P(('ctx', 'expert'))
- d_w_router: float32 [2048, 128], P(('ctx', 'expert'))
- d_w_gate: float32 [128, 2048, 768], P(('ctx', 'expert'))
- d_w_up: float32 [128, 2048, 768], P(('ctx', 'expert'))
- d_w_down: float32 [128, 768, 2048], P(('ctx', 'expert'))
The draws below stay inside these ranges and needn't reach their ends.
Inputs may be any that keep to these rules, and one draw needn't show every extreme that they name: `positions`: each sequence packs 3 documents end to end; a position is 0 at a document's first token and rises by one a token within it. One document of each sequence holds 192 tokens. `routes`: A token names 8 different experts; the tokens of one device name every expert exactly 8 times.
All inputs are finite; a program needn't handle non-finite values.
Results may differ from the reference program's by a relative error of at most 0.04.
Values may be sent and summed in bfloat16 or wider, within the bound.
No kernel may reach another device: no remote copies, remote signals or barrier semaphores. Data moves between devices by JAX's collectives and lax.ppermute only.
A program may use at most 256 MiB of HBM per device.

```python
import math
import jax
import jax.numpy as jnp
import numpy as np
from jax import lax

D = 2048
HEADS = 32
KV = 4
HD = 128
FF = 768
TOP = 8
TOK_DEV = 128
DOCS = 3
LENGTH = 256
SEQS = 64
EXPERTS = 128
CAP = 8
N_CTX = 2
N_EXPERT = 64


def draw_positions(key, part):
    key = jax.random.fold_in(key, 7)
    short_total = TOK_DEV // 2
    long_length = LENGTH - short_total

    def one_row(row_key):
        cut_key, place_key = jax.random.split(row_key)
        inner = jax.random.permutation(cut_key, jnp.arange(1, short_total, dtype=jnp.int32))[:DOCS - 2]
        bounds = jnp.concatenate([jnp.zeros((1,), jnp.int32), jnp.sort(inner), jnp.full((1,), short_total, jnp.int32)])
        short_lengths = bounds[1:] - bounds[:-1]
        long_index = jax.random.randint(place_key, (), 0, DOCS).astype(jnp.int32)
        doc_index = jnp.arange(DOCS, dtype=jnp.int32)
        before = short_lengths[jnp.clip(doc_index, 0, DOCS - 2)]
        after = short_lengths[jnp.clip(doc_index - 1, 0, DOCS - 2)]
        doc_lengths = jnp.where(doc_index < long_index, before, jnp.where(doc_index == long_index, long_length, after))
        starts = jnp.cumsum(doc_lengths) - doc_lengths
        places = jnp.arange(LENGTH, dtype=jnp.int32)
        begins = jnp.max(jnp.where(starts[None, :] <= places[:, None], starts[None, :], 0), axis=1)
        return (places - begins).astype(jnp.int32)
    return jax.vmap(one_row)(jax.random.split(key, SEQS))


def steps_of(stream_key, extent, pieces, least, largest):
    factor_of = 1.0
    for axis_at, shards_of in pieces:
        draws = jax.random.uniform(jax.random.fold_in(jax.random.fold_in(stream_key, 6), axis_at), (shards_of,), jnp.float32, least / len(pieces), largest / len(pieces))
        factor_of = factor_of * jnp.repeat(jnp.exp(draws), extent[axis_at] // shards_of).reshape((-1,) + (1,) * (len(extent) - 1 - axis_at))
    return factor_of


def shared_out(rng, own, number, rows, number_of, top, most, lean):
    ranking = jax.random.permutation(rng, number_of)
    heavy_load, common = shares(number_of, rows * top, most, lean, True), shares(number_of, rows * top, most, lean, False)
    places = jnp.arange(number_of)

    def named(tallies, turn):
        used = int((tallies > 0).sum())
        fixed = max(1, used // 4)
        moved = fixed + (places - fixed + turn * (used - fixed)) % max(1, number_of - fixed)
        return jnp.zeros((number_of,), jnp.int32).at[ranking[jnp.where(places < fixed, places, moved)]].set(jnp.asarray(tallies, jnp.int32))

    tallies = jnp.where(number % 4 == 0, named(heavy_load, number // 4), named(common, number - number // 4 - 1))
    mixed = jax.random.permutation(jax.random.fold_in(own, 3), number_of)
    donor, sink = mixed[0:number_of // 2 * 2:2], mixed[1:number_of // 2 * 2:2]
    slack = jnp.minimum(tallies[donor] - 1, most - tallies[sink]) // 2
    slack = jnp.where((donor == ranking[0]) | (sink == ranking[0]) | (tallies[sink] == 0), 0, jnp.maximum(slack, 0))
    moved = jax.random.randint(jax.random.fold_in(own, 4), (number_of // 2,), 0, 1 << 20) % (slack + 1)
    tallies = tallies.at[donor].add(-moved).at[sink].add(moved)
    items = jnp.searchsorted(jnp.cumsum(tallies), jnp.arange(rows * top), side="right").astype(jnp.int32)
    grid = items.reshape(top, rows).T
    grid = grid[jax.random.permutation(jax.random.fold_in(own, 1), rows)]
    turn = jax.random.randint(jax.random.fold_in(own, 2), (rows, 1), 0, top)
    return jnp.take_along_axis(grid, (jnp.arange(top)[None, :] + turn) % top, axis=1)


def shares(count, total, limit, lean, full):
    loads = [(1 << 20) // math.isqrt(rank ** lean) + 1 for rank in range(1, count + 1)]
    largest = limit if full else min(limit, max(-(-total // count), total * loads[0] // sum(loads)))
    least = 1 if total - largest >= count - 1 else 0
    counts, spare = [largest] + [least] * (count - 1), total - largest - least * (count - 1)
    while spare > 0:
        movable = [i for i in range(1, count) if counts[i] < largest] or [i for i in range(1, count) if counts[i] < limit]
        pool, left = sum([loads[i] for i in movable]), spare
        for i in movable:
            addition = min(limit - counts[i], max(1, left * loads[i] // pool), spare)
            counts[i] = counts[i] + addition
            spare = spare - addition
    return np.array(counts)


def centred(stream_key, dims, width, most, shards=(), kind=jnp.bfloat16):
    values = width * jax.random.normal(stream_key, dims, jnp.float32)
    if shards:
        values = values * steps_of(stream_key, dims, shards, -0.22, 0.18)
    return jnp.clip(values, -most, most).astype(kind)


def setup_inputs(seed: int = 0) -> dict:
    streams_of = jax.random.split(jax.random.key(seed), 17)
    tokens = centred(streams_of[0], (SEQS, LENGTH, D), 1.0, 6.0, ((0, 64), (1, 2)))
    positions = draw_positions(jax.random.fold_in(streams_of[16], 71), 0)
    routes_keys = jax.random.split(jax.random.fold_in(streams_of[2], 1), SEQS * LENGTH // TOK_DEV)
    routes_turns = jax.random.permutation(jax.random.fold_in(streams_of[2], 3), SEQS * LENGTH // TOK_DEV)
    routes = jax.vmap(lambda own, number: shared_out(jax.random.fold_in(streams_of[2], 2), own, number, TOK_DEV, EXPERTS, TOP, CAP, 0))(routes_keys, routes_turns).reshape((SEQS, LENGTH, TOP))
    attn_gain = jnp.clip(1.0 + 0.1 * jax.random.normal(streams_of[3], (D,), jnp.float32), 0.5, 1.5).astype(jnp.bfloat16)
    w_query = centred(streams_of[4], (D, HEADS * HD), D ** -0.5, 0.125, ((0, 128),))
    w_key = centred(streams_of[5], (D, KV * HD), D ** -0.5, 0.125, ((0, 128),))
    w_value = centred(streams_of[6], (D, KV * HD), D ** -0.5, 0.125, ((0, 128),))
    query_gain = jnp.clip(1.0 + 0.18 * jax.random.normal(streams_of[7], (HD,), jnp.float32), 0.099609375, 1.8984375).astype(jnp.bfloat16)
    key_gain = jnp.clip(1.0 + 0.18 * jax.random.normal(streams_of[8], (HD,), jnp.float32), 0.099609375, 1.8984375).astype(jnp.bfloat16)
    w_out = centred(streams_of[9], (HEADS * HD, D), (HEADS * HD // 16) ** -0.5, 0.375, ((0, 128),))
    ffn_gain = jnp.clip(1.0 + 0.1 * jax.random.normal(streams_of[10], (D,), jnp.float32), 0.5, 1.5).astype(jnp.bfloat16)
    w_router = centred(streams_of[11], (D, EXPERTS), (4 * D) ** -0.5, 0.0625, ((0, 128),))
    w_gate = centred(streams_of[12], (EXPERTS, D, FF), D ** -0.5, 0.125, ((0, 128),))
    w_up = centred(streams_of[13], (EXPERTS, D, FF), D ** -0.5, 0.125, ((0, 128),))
    w_down = centred(streams_of[14], (EXPERTS, FF, D), (FF // 16) ** -0.5, 0.875, ((0, 128),))
    cotangent = centred(streams_of[15], (SEQS, LENGTH, D), 1.0, 6.0, ((0, 64), (1, 2)))
    return {"tokens": tokens, "positions": positions, "routes": routes, "attn_gain": attn_gain, "w_query": w_query, "w_key": w_key, "w_value": w_value, "query_gain": query_gain, "key_gain": key_gain, "w_out": w_out, "ffn_gain": ffn_gain, "w_router": w_router, "w_gate": w_gate, "w_up": w_up, "w_down": w_down, "cotangent": cotangent}


@jax.custom_vjp
def low(v):
    return lax.optimization_barrier(v.astype(jnp.bfloat16)).astype(jnp.float32)

@jax.custom_vjp
def low_back(v):
    return v

def low_keep(v):
    return (low(v), None)

def low_pass(kept, grad):
    return (grad,)

def back_keep(v):
    return (v, None)

def back_low(kept, grad):
    return (low(grad),)
low.defvjp(low_keep, low_pass)
low_back.defvjp(back_keep, back_low)
epsilon = 1e-06
rope_base = 1000000.0
highest = lax.Precision.HIGHEST

def matmul(left, right):
    return jnp.dot(left, right, precision=highest, preferred_element_type=jnp.float32)

def rms_norm(values, scaling):
    inv_rms = lax.rsqrt(lax.optimization_barrier(jnp.mean(values * values, axis=-1, keepdims=True)) + epsilon)
    return values * inv_rms * scaling

def rotary(values, places):
    half_size = values.shape[-1] // 2
    frequency = rope_base ** (-(2.0 / values.shape[-1]) * jnp.arange(half_size, dtype=jnp.float32))
    angles = places.astype(jnp.float32)[:, None] * frequency[None, :]
    cosines = jnp.cos(angles)[:, None, :]
    sines = jnp.sin(angles)[:, None, :]
    first_half = values[..., :half_size]
    second_half = values[..., half_size:]
    return jnp.concatenate([first_half * cosines - second_half * sines, second_half * cosines + first_half * sines], axis=-1)

def attend(weights, sequence, places):
    w_query, w_key, w_value, query_gain, key_gain, w_out, attn_gain = weights
    normed = low(rms_norm(sequence, attn_gain))
    query_raw = low_back(matmul(normed, w_query)).reshape(LENGTH, HEADS, HD)
    key_raw = low_back(matmul(normed, w_key)).reshape(LENGTH, KV, HD)
    values = low(low_back(matmul(normed, w_value))).reshape(LENGTH, KV, HD)
    queries = low(rotary(rms_norm(query_raw, query_gain), places)).reshape(LENGTH, KV, HEADS // KV, HD)
    key_vecs = low(rotary(rms_norm(key_raw, key_gain), places))
    token_order = jnp.arange(LENGTH, dtype=jnp.int32)
    visible_pairs = (token_order[None, :] <= token_order[:, None]) & (token_order[:, None] - token_order[None, :] == places[:, None] - places[None, :])
    scores = jnp.einsum('qkgd,tkd->kgqt', queries, key_vecs, precision=highest) * HD ** (-0.5)
    scores = low_back(jnp.where(visible_pairs[None, None], scores, -1e+30))
    soft_weights = low(jax.nn.softmax(scores, axis=-1))
    mixture = jnp.einsum('kgqt,tkd->qkgd', soft_weights, values, precision=highest).reshape(LENGTH, HEADS * HD)
    mixture = low(low_back(mixture))
    return sequence + low_back(matmul(mixture, w_out))

def reference(tokens, positions, routes, attn_gain, w_query, w_key, w_value, query_gain, key_gain, w_out, ffn_gain, w_router, w_gate, w_up, w_down, cotangent):
    devices_all = N_CTX * N_EXPERT
    route_dev = routes.reshape(SEQS, N_CTX, TOK_DEV * TOP).transpose(1, 0, 2).reshape(devices_all, TOK_DEV * TOP)
    onehot = (route_dev[:, :, None] == jnp.arange(EXPERTS, dtype=jnp.int32)[None, None, :]).astype(jnp.int32)
    slot_rank = lax.optimization_barrier(jnp.sum((jnp.cumsum(onehot, axis=1) - 1) * onehot, axis=2))
    device_ids = jnp.arange(devices_all, dtype=jnp.int32)[:, None]
    slot_place = ((route_dev * devices_all + device_ids) * CAP + slot_rank).reshape(-1).astype(jnp.int32)
    source_row = jnp.zeros((EXPERTS * devices_all * CAP,), jnp.int32).at[slot_place].set(jnp.arange(devices_all * TOK_DEV * TOP, dtype=jnp.int32) // TOP)
    routes_flat = route_dev.reshape(-1, TOP)

    def forward(tokens_float, attn_scaling, query_w, key_w, value_w, query_scaling, key_scaling, out_w, ffn_scaling, router_w, gate_w, up_w, down_w):
        weights = (query_w, key_w, value_w, query_scaling, key_scaling, out_w, attn_scaling)

        def one_sequence(bundle):
            return attend(weights, bundle[0], bundle[1])
        after_attn = lax.map(jax.checkpoint(one_sequence), (tokens_float, positions))
        regrouped = after_attn.reshape(SEQS, N_CTX, TOK_DEV, D).transpose(1, 0, 2, 3).reshape(-1, D)
        normed = low(rms_norm(regrouped, ffn_scaling))
        logits = matmul(normed, router_w)
        chosen = jnp.take_along_axis(logits, routes_flat, axis=1)
        gate_weights = jax.nn.softmax(chosen, axis=-1)

        def one_expert(bundle):
            gate_one, up_one, down_one, rows_index = bundle
            inputs = low_back(normed[rows_index])
            gate_pre = low_back(matmul(inputs, gate_one))
            up_pre = low_back(matmul(inputs, up_one))
            hidden = low(jax.nn.silu(gate_pre) * up_pre)
            return low(low_back(matmul(hidden, down_one)))
        expert_rows = lax.map(jax.checkpoint(one_expert), (gate_w, up_w, down_w, source_row.reshape(EXPERTS, devices_all * CAP)))
        outputs_flat = expert_rows.reshape(-1, D)

        def combine_block(bundle):
            places_block, gates_block = bundle
            return lax.optimization_barrier(jnp.sum(gates_block[:, :, None] * outputs_flat[places_block], axis=1))
        mixture = lax.map(combine_block, (slot_place.reshape(devices_all, TOK_DEV, TOP), gate_weights.reshape(devices_all, TOK_DEV, TOP)))
        result = regrouped + mixture.reshape(-1, D)
        return result.reshape(N_CTX, SEQS, TOK_DEV, D).transpose(1, 0, 2, 3).reshape(SEQS, LENGTH, D)
    inputs_float = (tokens.astype(jnp.float32), attn_gain.astype(jnp.float32), w_query.astype(jnp.float32), w_key.astype(jnp.float32), w_value.astype(jnp.float32), query_gain.astype(jnp.float32), key_gain.astype(jnp.float32), w_out.astype(jnp.float32), ffn_gain.astype(jnp.float32), w_router.astype(jnp.float32), w_gate.astype(jnp.float32), w_up.astype(jnp.float32), w_down.astype(jnp.float32))
    block_out, pullback = jax.vjp(forward, *inputs_float)
    gradients = pullback(cotangent.astype(jnp.float32))
    return (block_out, gradients[0], gradients[1], gradients[2], gradients[3], gradients[4], gradients[5], gradients[6], gradients[7], gradients[8], gradients[9], gradients[10], gradients[11], gradients[12])
```

```python
from functools import partial

import jax
import jax.numpy as jnp
from jax import lax
from jax.experimental import pallas as pl
from jax.experimental.pallas import tpu as pltpu
from jax.sharding import Mesh
from jax.sharding import PartitionSpec as P

D = 2048
HEADS = 32
KV = 4
HD = 128
FF = 768
TOP = 8
TOK = 128
EXPERTS = 128
CAP = 8
WIDE = D + 128

epsilon = 1e-06
rope_base = 1000000.0
masked_score = -1e30
score_scale = HD ** (-0.5)
f32 = jnp.float32
bf16 = jnp.bfloat16
EXP = ("z", "x", "y")
ALL = ("ctx", "z", "x", "y")
SWAP = [(0, 1), (1, 0)]


def dot(a, b):
    return lax.dot_general(a, b, (((1,), (0,)), ((), ())), preferred_element_type=f32)


def dot_nt(a, b):
    return lax.dot_general(a, b, (((1,), (1,)), ((), ())), preferred_element_type=f32)


def dot_tn(a, b):
    return lax.dot_general(a, b, (((0,), (0,)), ((), ())), preferred_element_type=f32)


def call(body, grid, in_specs, out_specs, out_shape, scratch=(), flops=0, moved=0, vmem=40):
    return pl.pallas_call(
        body,
        grid=grid,
        in_specs=in_specs,
        out_specs=out_specs,
        out_shape=out_shape,
        scratch_shapes=list(scratch),
        compiler_params=pltpu.CompilerParams(vmem_limit_bytes=vmem * 2**20),
        cost_estimate=pl.CostEstimate(flops=flops, bytes_accessed=moved, transcendentals=0),
    )


def whole(shape):
    return pl.BlockSpec(shape, lambda *_: (0,) * len(shape))


def shape_of(dims, kind):
    return jax.ShapeDtypeStruct(dims, kind)


SIDE = 2 * 4 * TOK
COLS = 4 * HD + 2 * HD


def chunk_of(w_ref, count):
    return jnp.concatenate(
        [w_ref[:, 16 * k : 16 * k + 16, :].reshape(256, COLS) for k in range(count)], axis=0
    )


def project_body(x_ref, inv_ref, gain_ref, w_ref, raw_ref, normed_ref):
    x = x_ref[...].reshape(SIDE, 512).astype(f32)
    normed = (x * inv_ref[...] * gain_ref[...]).astype(bf16)
    normed_ref[...] = normed
    part = dot(normed, chunk_of(w_ref, 2)).reshape(2, 4 * TOK, COLS)

    @pl.when(pl.program_id(0) == 0)
    def _():
        raw_ref[...] = part

    @pl.when(pl.program_id(0) > 0)
    def _():
        raw_ref[...] += part


def project(x_all, inv, gain, gathered):
    return call(
        project_body,
        (4,),
        [
            pl.BlockSpec((2, 4 * TOK, 512), lambda i: (0, 0, i)),
            whole((SIDE, 1)),
            pl.BlockSpec((1, 512), lambda i: (0, i)),
            pl.BlockSpec((16, 32, COLS), lambda i: (0, i, 0)),
        ],
        [whole((2, 4 * TOK, COLS)), pl.BlockSpec((SIDE, 512), lambda i: (0, i))],
        [shape_of((2, 4 * TOK, COLS), f32), shape_of((SIDE, D), bf16)],
        flops=2 * SIDE * D * COLS,
        moved=14 * 2**20,
    )(x_all, inv, gain, gathered)


def prepared(raw, gain, cosines, sines):
    inv = lax.rsqrt(jnp.mean(raw * raw, axis=-1, keepdims=True) + epsilon)
    normed = raw * inv * gain
    return normed * cosines + pltpu.roll(normed, HD // 2, 1) * sines


def prepared_back(d_rot, raw, gain, cosines, sines):
    inv = lax.rsqrt(jnp.mean(raw * raw, axis=-1, keepdims=True) + epsilon)
    unit = raw * inv
    d_normed = d_rot * cosines + pltpu.roll(d_rot * sines, HD // 2, 1)
    d_gain = jnp.sum(d_normed * unit, axis=0, keepdims=True)
    d_unit = d_normed * gain
    d_raw = inv * (d_unit - unit * jnp.mean(unit * d_unit, axis=-1, keepdims=True))
    return d_raw, d_gain


def softmax_of(query, key, bias):
    scores = dot_nt(query, key) * score_scale + bias
    weight = jnp.exp(scores - jnp.max(scores, axis=-1, keepdims=True))
    return weight * (1.0 / jnp.sum(weight, axis=-1, keepdims=True))


def stacked(x, count=4):
    return jnp.concatenate([x[:, h * HD : (h + 1) * HD] for h in range(count)], axis=0)


def attend_body(raw_ref, bias_ref, cos_ref, sin_ref, qg, kg, q_out, k_out, v_out, mixed_out):
    def of(ref):
        return ref[...].reshape(2 * TOK, ref.shape[-1])

    cosines, sines = of(cos_ref), of(sin_ref)
    raw = of(raw_ref)
    key = prepared(raw[:, 512:640], kg[...], cosines, sines).astype(bf16)
    value = raw[:, 640:768].astype(bf16)
    k_out[...] = key.reshape(2, TOK, HD)
    v_out[...] = value.reshape(2, TOK, HD)
    cosines, sines = (jnp.concatenate([t] * 4, axis=0) for t in (cosines, sines))
    query = prepared(stacked(raw), qg[...], cosines, sines).astype(bf16)
    probs = softmax_of(query, key, jnp.concatenate([bias_ref[0]] * 4, axis=0))
    mixed = dot(probs.astype(bf16), value).astype(bf16)
    for h in range(4):
        at, rows = slice(h * HD, (h + 1) * HD), slice(h * 2 * TOK, (h + 1) * 2 * TOK)
        q_out[:, :, at] = query[rows].reshape(2, TOK, HD)
        mixed_out[:, :, at] = mixed[rows].reshape(2, TOK, HD)


def by_sequence(width):
    return pl.BlockSpec((2, TOK, width), lambda r: (0, r, 0))


def rows_of(width, kind=bf16):
    return shape_of((2, 4 * TOK, width), kind)


def attend(raw, bias, cosines, sines, qg, kg):
    one = pl.BlockSpec((1, 2 * TOK, 2 * TOK), lambda r: (r, 0, 0))
    return call(
        attend_body,
        (4,),
        [by_sequence(COLS), one, by_sequence(HD), by_sequence(HD)] + [whole((1, HD))] * 2,
        [by_sequence(512), by_sequence(HD), by_sequence(HD), by_sequence(512)],
        [rows_of(512), rows_of(HD), rows_of(HD), rows_of(512)],
        flops=4 * 16 * 256 * 256 * 128,
        moved=8 * 2**20,
    )(raw, bias, cosines, sines, qg, kg)


def attend_back_body(
    raw_ref, q_ref, k_ref, v_ref, dm_ref, bias_ref, cos_ref, sin_ref, qg, kg,
    d_out, gq_out, gk_out,
):
    def of(ref):
        return ref[...].reshape(2 * TOK, ref.shape[-1])

    @pl.when(pl.program_id(0) == 0)
    def _():
        gq_out[...] = jnp.zeros_like(gq_out)
        gk_out[...] = jnp.zeros_like(gk_out)

    cosines, sines = of(cos_ref), of(sin_ref)
    raw, key, value = of(raw_ref), of(k_ref), of(v_ref)
    query, d_mixed = stacked(of(q_ref)), stacked(of(dm_ref))
    probs = softmax_of(query, key, jnp.concatenate([bias_ref[0]] * 4, axis=0))
    d_probs = dot_nt(d_mixed, value)
    d_value = dot_tn(probs.astype(bf16), d_mixed)
    spread = probs * d_probs
    d_scores = (spread - probs * jnp.sum(spread, axis=-1, keepdims=True)).astype(bf16)
    d_query = dot(d_scores, key) * score_scale
    d_key = dot_tn(d_scores, query)
    cos_all, sin_all = (jnp.concatenate([t] * 4, axis=0) for t in (cosines, sines))
    d_raw, gain_sum = prepared_back(d_query, stacked(raw), qg[...], cos_all, sin_all)
    d_raw = d_raw.astype(bf16)
    for h in range(4):
        at, rows = slice(h * HD, (h + 1) * HD), slice(h * 2 * TOK, (h + 1) * 2 * TOK)
        d_out[:, :, at] = d_raw[rows].reshape(2, TOK, HD)
    d_raw, d_gain = prepared_back(d_key * score_scale, raw[:, 512:640], kg[...], cosines, sines)
    d_out[:, :, 512:640] = d_raw.astype(bf16).reshape(2, TOK, HD)
    d_out[:, :, 640:768] = d_value.astype(bf16).reshape(2, TOK, HD)
    gq_out[...] += gain_sum
    gk_out[...] += d_gain


def attend_back(raw, query, key, value, d_mixed, bias, cosines, sines, qg, kg):
    one = pl.BlockSpec((1, 2 * TOK, 2 * TOK), lambda r: (r, 0, 0))
    return call(
        attend_back_body,
        (4,),
        [by_sequence(COLS), by_sequence(512), by_sequence(HD), by_sequence(HD), by_sequence(512)]
        + [one, by_sequence(HD), by_sequence(HD)]
        + [whole((1, HD))] * 2,
        [by_sequence(COLS), whole((1, HD)), whole((1, HD))],
        [rows_of(COLS), shape_of((1, HD), f32), shape_of((1, HD), f32)],
        flops=10 * 16 * 256 * 256 * 128,
        moved=10 * 2**20,
    )(raw, query, key, value, d_mixed, bias, cosines, sines, qg, kg)


def out_body(m_ref, w_ref, o_ref):
    o_ref[...] = dot(m_ref[0], w_ref[...].reshape(512, 1024)).astype(o_ref.dtype)


def out_project(mixed, gathered, half, kind):
    return call(
        out_body,
        (2,),
        [
            pl.BlockSpec((1, 512, 512), lambda j: (half, 0, 0)),
            pl.BlockSpec((16, 32, 1024), lambda j: (0, 4 + j, 0)),
        ],
        pl.BlockSpec((512, 1024), lambda j: (0, j)),
        shape_of((512, D), kind),
        flops=2 * 512 * 512 * 2048,
        moved=6 * 2**20,
    )(mixed, gathered)


def out_back_body(d_ref, w_ref, o_ref):
    w = w_ref[...]
    low = w[:, :32].reshape(512, 1024)
    high = w[:, 32:].reshape(512, 1024)
    o_ref[...] = (dot_nt(d_ref[:, :1024], low) + dot_nt(d_ref[:, 1024:], high)).astype(bf16)


def out_back(d_side, gathered):
    return call(
        out_back_body,
        (2,),
        [
            pl.BlockSpec((256, D), lambda i: (i, 0)),
            pl.BlockSpec((16, 64, 1024), lambda i: (0, 2, 0)),
        ],
        pl.BlockSpec((256, 512), lambda i: (i, 0)),
        shape_of((512, 512), bf16),
        flops=2 * 512 * 512 * 2048,
        moved=5 * 2**20,
    )(d_side, gathered)


def out_grad_body(m_ref, a_ref, b_ref, o_ref):
    o_ref[...] = (dot_tn(m_ref[0], a_ref[...]) + dot_tn(m_ref[1], b_ref[...])).astype(bf16)


def out_grad(mixed, d_side, d_other):
    block = pl.BlockSpec((512, 1024), lambda j: (0, j))
    return call(
        out_grad_body,
        (2,),
        [whole((2, 512, 512)), block, block],
        block,
        shape_of((512, D), bf16),
        flops=2 * 1024 * 512 * 2048,
        moved=7 * 2**20,
    )(mixed, d_side, d_other)


def two_halves(value):
    high = value.astype(bf16)
    low = (value - high.astype(f32)).astype(bf16)
    lane = lax.broadcasted_iota(jnp.int32, (value.shape[0], 128), 1)
    return jnp.where(lane < 64, high.astype(f32), low.astype(f32)).astype(bf16)


def dispatch_body(
    x_ref, own_ref, left_ref, right_ref, gain_ref, router_ref, named_ref, place_ref,
    after_ref, low_ref, gate_ref, send_ref, turned,
):
    @pl.when(pl.program_id(0) == 0)
    def _():
        moved = left_ref[...].astype(f32) + right_ref[...].astype(f32)
        after = x_ref[...].astype(f32) + (own_ref[...] + moved)
        after_ref[...] = after
        inv = lax.rsqrt(jnp.mean(after * after, axis=-1, keepdims=True) + epsilon)
        low = (after * inv * gain_ref[...]).astype(bf16)
        low_ref[...] = low
        logits = dot(low, router_ref[...])
        named = named_ref[...]
        kept = jnp.where(named > 0.0, logits, masked_score)
        weight = jnp.exp(kept - jnp.max(kept, axis=-1, keepdims=True)) * named
        gates = weight * (1.0 / jnp.sum(weight, axis=-1, keepdims=True))
        gate_ref[...] = gates
        turned[...] = gates.T

    place = place_ref[...]
    send_ref[:, :D] = dot(place, low_ref[...]).astype(bf16)
    at = pl.multiple_of(pl.program_id(0) * 16, 16)
    gates = turned[pl.ds(at, 16), :]
    spread = jnp.broadcast_to(gates[:, None, :], (16, 8, 128)).reshape(128, 128)
    send_ref[:, D:] = two_halves(jnp.sum(spread * place.astype(f32), axis=-1, keepdims=True))


def dispatch(x, own, left, right, gain, router, named, place):
    row = whole((TOK, D))
    return call(
        dispatch_body,
        (8,),
        [row, row, row, row, whole((1, D)), whole((D, 128)), whole((128, 128))]
        + [pl.BlockSpec((128, 128), lambda i: (i, 0))],
        [row, row, whole((128, 128)), pl.BlockSpec((128, WIDE), lambda i: (i, 0))],
        [
            shape_of((TOK, D), f32),
            shape_of((TOK, D), bf16),
            shape_of((128, 128), f32),
            shape_of((1024, WIDE), bf16),
        ],
        scratch=[pltpu.VMEM((128, 128), f32)],
        flops=2 * 1024 * 128 * 2048,
        moved=9 * 2**20,
    )(x, own, left, right, gain, router, named, place)


def expert_body(
    x_ref, dh_ref, wg_ref, wu_ref, rows_ref, hid_ref, hidw_ref, dg_ref, du_ref
):
    x = x_ref[:, :D]
    side = x_ref[:, D:].astype(f32)
    gate_weight = side[:, 0:1] + side[:, 64:65]
    gate = dot(x, wg_ref[...])
    up = dot(x, wu_ref[...])
    sig = 1.0 / (1.0 + jnp.exp(-gate))
    act = gate * sig
    hidden = (act * up).astype(bf16)
    hid_ref[...] = hidden
    hidden = hidden.astype(f32)
    hidw_ref[...] = (hidden * gate_weight).astype(bf16)
    d_hidden = dh_ref[...]
    rows_ref[:, D:] = two_halves(jnp.sum(hidden * d_hidden, axis=-1, keepdims=True))
    d_hidden = d_hidden * gate_weight
    d_gate = (d_hidden * up * sig * (1.0 + gate * (1.0 - sig))).astype(bf16)
    d_up = (d_hidden * act).astype(bf16)
    dg_ref[...] = d_gate
    du_ref[...] = d_up
    rows_ref[:, :D] = (dot_nt(d_gate, wg_ref[...]) + dot_nt(d_up, wu_ref[...])).astype(bf16)


def expert(rows, d_hidden, w_gate, w_up):
    wide = pl.BlockSpec((256, WIDE), lambda i: (i, 0))
    inner = pl.BlockSpec((256, FF), lambda i: (i, 0))
    return call(
        expert_body,
        (4,),
        [wide, inner, whole((D, FF)), whole((D, FF))],
        [wide, inner, inner, inner, inner],
        [shape_of((1024, WIDE), bf16)] + [shape_of((1024, FF), bf16)] * 4,
        flops=8 * 1024 * 2048 * 768,
        moved=24 * 2**20,
        vmem=48,
    )(rows, d_hidden, w_gate, w_up)


def in_grad_body(x_ref, dg_ref, du_ref, gate_ref, up_ref):
    gate_ref[...] = dot_tn(x_ref[...], dg_ref[...])
    up_ref[...] = dot_tn(x_ref[...], du_ref[...])


def in_grads(rows, d_gate, d_up):
    out = pl.BlockSpec((256, FF), lambda i: (i, 0))
    return call(
        in_grad_body,
        (8,),
        [pl.BlockSpec((1024, 256), lambda i: (0, i)), whole((1024, FF)), whole((1024, FF))],
        [out, out],
        [shape_of((D, FF), f32)] * 2,
        flops=4 * 1024 * 2048 * 768,
        moved=20 * 2**20,
    )(rows, d_gate, d_up)


def down_grad_body(h_ref, g_ref, o_ref):
    o_ref[...] = dot_tn(h_ref[...], g_ref[...])


def down_grad(hidden, g_rows):
    return call(
        down_grad_body,
        (4,),
        [whole((1024, FF)), pl.BlockSpec((1024, 512), lambda i: (0, i))],
        pl.BlockSpec((FF, 512), lambda i: (0, i)),
        shape_of((FF, D), f32),
        flops=2 * 1024 * 2048 * 768,
        moved=12 * 2**20,
    )(hidden, g_rows)


def combine_body(
    back_ref, turn_ref, gates_ref, after_ref, low_ref, gain_ref, router_ref, g_ref,
    d_after_ref, d_low_ref, d_router_ref, d_gain_ref, total, d_gates,
):
    step = pl.program_id(0)

    @pl.when(step == 0)
    def _():
        total[...] = jnp.zeros_like(total)
        d_gates[...] = jnp.zeros_like(d_gates)

    turn = turn_ref[...]
    total[...] += dot(turn, back_ref[:, :D])
    side = back_ref[:, D:].astype(f32)
    slot = lax.broadcasted_iota(jnp.int32, (256, 128), 0) + step * 256
    named = (slot // CAP) == lax.broadcasted_iota(jnp.int32, (256, 128), 1)
    high = jnp.where(named, side[:, 0:1], 0.0).astype(bf16)
    low = jnp.where(named, side[:, 64:65], 0.0).astype(bf16)
    d_gates[...] += dot(turn, high) + dot(turn, low)

    @pl.when(step == 3)
    def _():
        gates, got = gates_ref[...], d_gates[...]
        d_logits = gates * (got - jnp.sum(gates * got, axis=-1, keepdims=True))
        d_high = d_logits.astype(bf16)
        d_rest = (d_logits - d_high.astype(f32)).astype(bf16)
        router = router_ref[...]
        d_normed = total[...] + (dot_nt(d_high, router) + dot_nt(d_rest, router))
        rows = low_ref[...]
        d_router_ref[...] = dot_tn(rows, d_high) + dot_tn(rows, d_rest)
        after = after_ref[...]
        inv = lax.rsqrt(jnp.mean(after * after, axis=-1, keepdims=True) + epsilon)
        unit = after * inv
        d_gain_ref[...] = jnp.sum(d_normed * unit, axis=0, keepdims=True)
        d_unit = d_normed * gain_ref[...]
        d_after = g_ref[...].astype(f32) + inv * (
            d_unit - unit * jnp.mean(unit * d_unit, axis=-1, keepdims=True)
        )
        d_after_ref[...] = d_after
        d_low_ref[...] = d_after.astype(bf16)


def combine(back, turn, gates, after, low, gain, router, g):
    row = whole((TOK, D))
    return call(
        combine_body,
        (4,),
        [
            pl.BlockSpec((256, WIDE), lambda i: (i, 0)),
            pl.BlockSpec((128, 256), lambda i: (0, i)),
            whole((128, 128)),
            row,
            row,
            whole((1, D)),
            whole((D, 128)),
            row,
        ],
        [row, row, whole((D, 128)), whole((1, D))],
        [
            shape_of((TOK, D), f32),
            shape_of((TOK, D), bf16),
            shape_of((D, 128), f32),
            shape_of((1, D), f32),
        ],
        scratch=[pltpu.VMEM((TOK, D), f32), pltpu.VMEM((128, 128), f32)],
        flops=2 * 1024 * 128 * 2048,
        moved=9 * 2**20,
    )(back, turn, gates, after, low, gain, router, g)


def project_back_body(d_ref, w_ref, x_ref, inv_ref, own_ref, send_ref, gain_ref):
    part = dot_nt(d_ref[...].reshape(SIDE, COLS), chunk_of(w_ref, 2))
    own_ref[...] = part[:512]
    send_ref[...] = part[512:].astype(bf16)
    unit = x_ref[...].reshape(SIDE, 512).astype(f32) * inv_ref[...]
    gain_ref[...] = jnp.sum(part * unit, axis=0, keepdims=True)


def project_back(d_raw, gathered, x_all, inv):
    out = pl.BlockSpec((512, 512), lambda i: (0, i))
    return call(
        project_back_body,
        (4,),
        [
            whole((2, 512, COLS)),
            pl.BlockSpec((16, 32, COLS), lambda i: (0, i, 0)),
            pl.BlockSpec((2, 512, 512), lambda i: (0, 0, i)),
            whole((SIDE, 1)),
        ],
        [out, out, pl.BlockSpec((1, 512), lambda i: (0, i))],
        [shape_of((512, D), f32), shape_of((512, D), bf16), shape_of((1, D), f32)],
        flops=2 * SIDE * D * COLS,
        moved=14 * 2**20,
    )(d_raw, gathered, x_all, inv)


def project_grad_body(n_ref, d_ref, side_ref, o_ref):
    o_ref[:, :COLS] = dot_tn(n_ref[...], d_ref[...].reshape(SIDE, COLS)).astype(bf16)
    o_ref[:, COLS:] = side_ref[...].astype(bf16)


def project_grad(normed, d_raw, side):
    return call(
        project_grad_body,
        (4,),
        [
            pl.BlockSpec((SIDE, 512), lambda i: (0, i)),
            whole((2, 512, COLS)),
            pl.BlockSpec((512, 256), lambda i: (i, 0)),
        ],
        pl.BlockSpec((512, 1024), lambda i: (i, 0)),
        shape_of((D, 1024), bf16),
        flops=2 * SIDE * D * COLS,
        moved=10 * 2**20,
    )(normed, d_raw, side)


def grad_sum_body(x_ref, q_ref, kv_ref, rest_ref):
    total = jnp.sum(x_ref[0].astype(f32), axis=0)
    q_ref[...] = total[:, :512]

    @pl.when(pl.program_id(0) % 2 == 0)
    def _():
        kv_ref[0] = total[:, 512:COLS]

    @pl.when(pl.program_id(0) % 2 == 1)
    def _():
        kv_ref[0] += total[:, 512:COLS]

    @pl.when(pl.program_id(0) == 0)
    def _():
        rest_ref[...] = total[:, COLS:]

    @pl.when(pl.program_id(0) > 0)
    def _():
        rest_ref[...] += total[:, COLS:]


def grad_sum(parts):
    return call(
        grad_sum_body,
        (8,),
        [pl.BlockSpec((1, 16, 16, 1024), lambda i: (i, 0, 0, 0))],
        [
            pl.BlockSpec((16, 512), lambda i: (0, i)),
            pl.BlockSpec((1, 16, 256), lambda i: (i // 2, 0, 0)),
            whole((16, 256)),
        ],
        [shape_of((16, 4096), f32), shape_of((4, 16, 256), f32), shape_of((16, 256), f32)],
        moved=5 * 2**20,
    )(parts)


def around(step):
    return [(i, (i + step) % 4) for i in range(4)]


def ring_gather(x):
    h = x.shape[0] // 2
    after = lax.ppermute(x, "z", around(-1))
    before = lax.ppermute(x, "z", around(1))
    far_a = lax.ppermute(after[:h], "z", around(-1))
    far_b = lax.ppermute(before[h:], "z", around(1))
    return jnp.concatenate([x, after, far_a, far_b, before], axis=0)


def ring_sum(own, got):
    piece = [
        own[r * TOK : (r + 1) * TOK].astype(f32) + got[r * TOK : (r + 1) * TOK].astype(f32)
        for r in range(4)
    ]
    h = TOK // 2
    far = piece[2].astype(bf16)
    a = lax.ppermute(far[:h], "z", around(1))
    b = lax.ppermute(far[h:], "z", around(-1))
    right = jnp.concatenate([piece[1][:h] + a.astype(f32), piece[1][h:]], axis=0).astype(bf16)
    left = jnp.concatenate([piece[3][:h], piece[3][h:] + b.astype(f32)], axis=0).astype(bf16)
    return piece[0], lax.ppermute(right, "z", around(1)), lax.ppermute(left, "z", around(-1))


def local(
    tokens,
    positions,
    routes,
    attn_gain,
    w_query,
    w_key,
    w_value,
    query_gain,
    key_gain,
    w_out,
    ffn_gain,
    w_router,
    w_gate,
    w_up,
    w_down,
    cotangent,
):
    c = lax.axis_index("ctx")

    def swapped(x):
        return lax.ppermute(x, "ctx", SWAP)

    gain_columns = jnp.concatenate(
        [
            attn_gain[:, None],
            ffn_gain[:, None],
            jnp.pad(query_gain[:, None], ((0, 15), (0, 0))),
            jnp.pad(key_gain[:, None], ((0, 15), (0, 0))),
            jnp.zeros((16, 124), bf16),
        ],
        axis=1,
    )
    queries_of = w_query.reshape(16, 8, 512).transpose(1, 0, 2)
    keys_of = jnp.repeat(w_key.reshape(16, 4, HD).transpose(1, 0, 2), 2, axis=0)
    values_of = jnp.repeat(w_value.reshape(16, 4, HD).transpose(1, 0, 2), 2, axis=0)
    everyone = jnp.broadcast_to(
        jnp.concatenate([w_router, gain_columns], axis=1)[None], (8, 16, 256)
    )
    column = lax.all_to_all(
        jnp.concatenate([queries_of, keys_of, values_of, everyone], axis=2),
        ("ctx", "z"),
        0,
        0,
        tiled=True,
    )
    pack = jnp.concatenate([column.reshape(128, 1024), w_out[:, :1024], w_out[:, 1024:]], axis=0)
    gathered = lax.all_gather(pack, ("x", "y"), axis=0, tiled=False)

    x_own, g_own = tokens[0], cotangent[0]
    places_own = lax.dynamic_slice_in_dim(positions[0], c * TOK, TOK).astype(bf16)
    x_side = ring_gather(jnp.concatenate([x_own, jnp.tile(places_own[:, None], (1, 128))], axis=1))
    x_both = jnp.stack([x_side, swapped(x_side)])
    x_all, places = x_both[:, :, :D], x_both[:, :, D].astype(f32)
    x_float = x_all.astype(f32)
    inv = lax.rsqrt(jnp.mean(x_float * x_float, axis=-1) + epsilon)
    frequency = rope_base ** (-(2.0 / HD) * jnp.arange(HD // 2, dtype=f32))
    angles = places[:, :, None] * frequency
    cosines = jnp.concatenate([jnp.cos(angles)] * 2, axis=-1)
    sines = jnp.concatenate([-jnp.sin(angles), jnp.sin(angles)], axis=-1)
    line = jnp.arange(TOK, dtype=f32)
    order = jnp.concatenate([line + c * TOK, line + (1 - c) * TOK])
    places = places.reshape(2, 4, TOK).transpose(1, 0, 2).reshape(4, 2 * TOK)
    visible = (order[None, None, :] <= order[None, :, None]) & (
        order[None, :, None] - order[None, None, :] == places[:, :, None] - places[:, None, :]
    )
    bias = jnp.where(visible, 0.0, masked_score).astype(f32)
    inv = inv.reshape(SIDE, 1)

    named = jnp.sum(
        (routes[0][:, :, None] == jnp.arange(EXPERTS, dtype=jnp.int32)).astype(f32), axis=1
    )
    before = jnp.arange(TOK)[:, None] > jnp.arange(TOK)[None, :]
    rank = dot(before.astype(bf16), named.astype(bf16))
    slot_rank = jnp.arange(CAP, dtype=f32)
    turn = (
        (named[:, :, None] > 0.0) & (rank[:, :, None] == slot_rank[None, None, :])
    ).reshape(TOK, EXPERTS * CAP)
    turn = turn.astype(bf16)
    place = turn.T

    g_send = dot(place, g_own).astype(bf16).reshape(EXPERTS, CAP, D)
    g_rows = lax.all_to_all(g_send, ALL, 0, 0, tiled=True).reshape(-1, D)
    gate_local, up_local, down_local = w_gate[0], w_up[0], w_down[0]

    gathered, g_rows = lax.optimization_barrier((gathered, g_rows))
    d_hidden_raw = dot_nt(g_rows, down_local)
    small = gathered[:, :128, COLS:].reshape(16, 8, 16, 256).transpose(1, 0, 2, 3).reshape(D, 256)
    router_full = small[:, :128]
    gains = small[:, 128:132].astype(f32)
    attn_scale = gains[:, 0].reshape(1, D)
    ffn_scale = gains[:, 1].reshape(1, D)
    qg = gains[:, 2].reshape(HD, 16)[:, 0].reshape(1, HD)
    kg = gains[:, 3].reshape(HD, 16)[:, 0].reshape(1, HD)

    raw, normed = project(x_all, inv, attn_scale, gathered)
    query, key, value, mixed = attend(raw, bias, cosines, sines, qg, kg)
    out_got = swapped(out_project(mixed, gathered, 1, bf16))
    out_own = out_project(mixed, gathered, 0, f32)
    out_pieces = ring_sum(out_own, out_got)

    after, ffn_low, gates, send = dispatch(
        x_own, *out_pieces, ffn_scale, router_full, named, place
    )
    received = lax.all_to_all(send.reshape(EXPERTS, CAP, WIDE), ALL, 0, 0, tiled=True)
    received = received.reshape(-1, WIDE)
    d_rows, hidden, hidden_w, d_gate, d_up = expert(received, d_hidden_raw, gate_local, up_local)
    back = lax.all_to_all(d_rows.reshape(EXPERTS, CAP, WIDE), ALL, 0, 0, tiled=True)
    back = back.reshape(-1, WIDE)
    produced = dot(hidden, down_local).astype(bf16)
    grad_gate, grad_up = in_grads(received, d_gate, d_up)
    grad_down = down_grad(hidden_w, g_rows)

    d_after, d_attn, d_router, d_ffn_gain = combine(
        back, turn, gates, after, ffn_low, ffn_scale, router_full, g_own
    )
    d_side = ring_gather(d_attn)
    produced, d_side = lax.optimization_barrier((produced, d_side))
    returned = lax.all_to_all(produced.reshape(EXPERTS, CAP, D), ALL, 0, 0, tiled=True)
    returned = returned.reshape(-1, D)
    weighted = jnp.repeat(gates, CAP, axis=1) * turn.astype(f32)
    weighted_high = weighted.astype(bf16)
    weighted_rest = (weighted - weighted_high.astype(f32)).astype(bf16)
    block_out = after + (dot(weighted_high, returned) + dot(weighted_rest, returned))

    d_other = swapped(d_side)
    d_mixed = jnp.stack([out_back(d_side, gathered), out_back(d_other, gathered)])
    grad_out = out_grad(mixed, d_side, d_other)
    grad_out = lax.all_to_all(grad_out.reshape(16, 32, D), ("x", "y"), 0, 0, tiled=True)
    grad_out = jnp.sum(grad_out.astype(f32), axis=0)

    d_raw, d_query_gain, d_key_gain = attend_back(
        raw, query, key, value, d_mixed, bias, cosines, sines, qg, kg
    )
    d_own, d_send, d_attn_gain = project_back(d_raw, gathered, x_all, inv)
    d_pieces = ring_sum(d_own, swapped(d_send))
    d_normed = d_pieces[0] + d_pieces[1].astype(f32) + d_pieces[2].astype(f32)
    inv_own = inv[:TOK]
    unit = x_own.astype(f32) * inv_own
    d_unit = d_normed * attn_scale
    d_tokens = d_after + inv_own * (
        d_unit - unit * jnp.mean(unit * d_unit, axis=-1, keepdims=True)
    )

    per_chip = jnp.zeros((128, 16, 2), f32)
    per_chip = per_chip.at[:, 0, 0].set(d_query_gain[0]).at[:, 0, 1].set(d_key_gain[0])
    side = jnp.concatenate(
        [
            d_router,
            d_attn_gain.reshape(D, 1),
            d_ffn_gain.reshape(D, 1),
            per_chip.reshape(D, 2),
            jnp.zeros((D, 124), f32),
        ],
        axis=1,
    )
    sums = project_grad(normed, d_raw, side).reshape(128, 16, 1024)
    sums = lax.all_to_all(sums, ALL, 0, 0, tiled=True).reshape(8, 16, 16, 1024)
    grad_query, pair, rest = grad_sum(sums)
    grad_key = pair[:, :, :HD].transpose(1, 0, 2).reshape(16, 512)
    grad_value = pair[:, :, HD:].transpose(1, 0, 2).reshape(16, 512)

    return (
        block_out[None],
        d_tokens[None],
        rest[:, 128],
        grad_query,
        grad_key,
        grad_value,
        rest[0, 130:131],
        rest[0, 131:132],
        grad_out,
        rest[:, 129],
        rest[:, :128],
        grad_gate[None],
        grad_up[None],
        grad_down[None],
    )


def solution(mesh):
    chips = Mesh(mesh.devices.reshape(2, 4, 4, 4), ALL)
    tokens = P(EXP, "ctx", None)
    row = P(ALL, None)
    line = P(ALL)
    stack = P(ALL, None, None)
    placed = (
        tokens, P(EXP, None), tokens, line, row, row, row, line, line, row, line, row,
        stack, stack, stack, tokens,
    )
    given = (
        tokens, tokens, line, row, row, row, line, line, row, line, row, stack, stack, stack,
    )
    return jax.shard_map(local, mesh=chips, in_specs=placed, out_specs=given, check_vma=False)
```
